32 devices in a mesh: src: 8 (over z, x), snk: 2 (over y), mom: 2 (over core).
Axes of the slice: x: 2, y: 2, z: 4, core: 2. Of those that a mesh axis runs over, the one named last changes fastest.
Arguments:
- peramb: bfloat16 [24, 8, 256, 256], P(None, 'snk', 'src'), may hold values from -0.375 to 0.375
- elem_src: bfloat16 [24, 16, 256, 256], P('src', 'mom'), may hold values from -6 to 6
- elem_snk: bfloat16 [24, 16, 256, 256], P('src', 'mom'), may hold values from -6 to 6
- op_elem: int32 [64], replicated, may hold values from 0 to 15
- hlt_kernel: float32 [8, 128], replicated, may hold values from -2 to 2
Outputs:
- smeared: float32 [64, 16, 128], P('src', 'mom')
The draws below stay inside these ranges and needn't reach their ends.
All inputs are finite; a program needn't handle non-finite values.
Results may differ from the reference program's by a relative error of at most 0.004.
Values may be sent and summed in bfloat16 or wider, within the bound.
No kernel may reach another device: no remote copies, remote signals or barrier semaphores. Data moves between devices by JAX's collectives and lax.ppermute only.
A program may use at most 128 MiB of HBM per device.

```python
import math
import jax
import jax.numpy as jnp
from jax import lax

NV = 256
OPS = 64
NELEM = 16
NK = 128
NT0 = 24
NTS = 8


def plant(entries, rng, least, largest):
    extent = entries.shape
    index_at = [jax.random.randint(jax.random.fold_in(rng, axis), (), 0, extent[axis]) for axis in range(len(extent))]
    entries = entries.at[tuple(index_at)].set(least)
    longest = extent.index(max(extent))
    index_at[longest] = (index_at[longest] + 1) % extent[longest]
    return entries.at[tuple(index_at)].set(largest)


def block_levels(stream_key, shape, pieces, smallest, largest):
    factor_of, own = 1.0, jax.random.fold_in(stream_key, 6)
    for axis_at, blocks in pieces:
        heights = jnp.exp(jax.random.uniform(jax.random.fold_in(own, axis_at), (blocks,), jnp.float32, smallest / len(pieces), largest / len(pieces)))
        factor_of = factor_of * jnp.repeat(heights, shape[axis_at] // blocks).reshape([-1 if axis == axis_at else 1 for axis in range(len(shape))])
    return factor_of


def bell_draw(key, shape, deviation, bound, shards=(), kind=jnp.bfloat16):
    loudness = block_levels(key, shape, shards, -0.22, 0.18) if shards else 1.0
    entries = jax.random.normal(key, shape, jnp.float32) * deviation * loudness
    return jnp.minimum(jnp.maximum(entries, -bound), bound).astype(kind)


def setup_inputs(seed: int = 0) -> dict:
    keys = jax.random.split(jax.random.key(seed), 6)
    peramb = bell_draw(keys[0], (NT0, NTS, NV, NV), NV ** -0.5, 0.375, ((1, 2), (2, 8)))
    elem_src = bell_draw(keys[1], (NT0, NELEM, NV, NV), 1.0, 6.0, ((0, 8), (1, 2)))
    elem_snk = bell_draw(keys[2], (NT0, NELEM, NV, NV), 1.0, 6.0, ((0, 8), (1, 2)))
    op_elem = plant(jax.random.randint(keys[3], (OPS,), 0, NELEM), jax.random.fold_in(keys[3], 1), 0, NELEM - 1).astype(jnp.int32)
    hlt_kernel = bell_draw(keys[4], (NTS, NK), NTS ** -0.5, 2.0, (), jnp.float32)
    return {"peramb": peramb, "elem_src": elem_src, "elem_snk": elem_snk, "op_elem": op_elem, "hlt_kernel": hlt_kernel}


def reference(peramb, elem_src, elem_snk, op_elem, hlt_kernel):
    source_count = peramb.shape[0]
    sep_count = peramb.shape[1]
    eigen_count = peramb.shape[3]
    norm_factor = 1.0 / (eigen_count * math.sqrt(source_count))
    highest = lax.Precision.HIGHEST

    def one_source(inputs):
        propagator, source_elems, start = inputs
        sink_index = ((start + jnp.arange(sep_count, dtype=jnp.int32)) % source_count).astype(jnp.int32)
        sink_elems = jnp.take(elem_snk, sink_index, axis=0).astype(jnp.float32)
        prop_float = propagator.astype(jnp.float32)
        half_product = jnp.einsum('sab,fbc->sfac', prop_float, source_elems.astype(jnp.float32), precision=highest).astype(jnp.bfloat16)
        sandwich = jnp.einsum('sfac,sdc->sfad', half_product.astype(jnp.float32), prop_float, precision=highest).astype(jnp.bfloat16)
        return jnp.einsum('seab,sfab->sef', sink_elems, sandwich.astype(jnp.float32), precision=highest)
    traces = lax.map(one_source, (peramb, elem_src, jnp.arange(source_count, dtype=jnp.int32)))
    picked = traces[:, :, op_elem, :]
    correlator = jnp.transpose(lax.optimization_barrier(jnp.sum(picked, axis=0)), (1, 0, 2)) * norm_factor
    return jnp.einsum('otf,tk->ofk', correlator, hlt_kernel, precision=highest)
```

```python
import functools
import math

import jax
import jax.numpy as jnp
from jax import lax
from jax.experimental import pallas as pl
from jax.experimental.pallas import tpu as pltpu
from jax.sharding import PartitionSpec as P

BLK = 16
ANY = pl.BlockSpec(memory_space=pl.ANY)


def shifted(value, axis, steps):
    count = lax.axis_size(axis)
    pairs = [(source, (source + steps) % count) for source in range(count)]
    return lax.ppermute(value, axis, pairs)


def swapped(value, axis):
    count = lax.axis_size(axis)
    return lax.ppermute(value, axis, [(source, source ^ 1) for source in range(count)])


def copy_all(copies):
    for copy in copies:
        copy.start()
    for copy in copies:
        copy.wait()


def shear_kernel(n_src, own, seps, peramb_ref, out_ref, sems):
    source_count = peramb_ref.shape[0]
    sep_local = peramb_ref.shape[1]
    first = lax.axis_index("mom") * seps
    sep0 = lax.axis_index("snk") * sep_local + first
    copies = []
    for d in range(n_src):
        for j in range(own):
            for h in range(seps):
                start = lax.rem(own * d + j - h - sep0 + 2 * source_count, source_count)
                copies.append(
                    pltpu.make_async_copy(
                        peramb_ref.at[start, first + h], out_ref.at[d, j, h], sems.at[len(copies)]
                    )
                )
    copy_all(copies)


def shear(peramb, n_src, own, seps):
    rows, cols = peramb.shape[2:]
    return pl.pallas_call(
        functools.partial(shear_kernel, n_src, own, seps),
        out_shape=jax.ShapeDtypeStruct((n_src, own, seps, rows, cols), peramb.dtype),
        in_specs=[ANY],
        out_specs=ANY,
        scratch_shapes=[pltpu.SemaphoreType.DMA((n_src * own * seps,))],
    )(peramb)


def trace_kernel(units, own, nf, n_sep, perm_parts, elem_parts, n_slices, *refs):
    refs = list(refs)
    p_in = [refs.pop(0) for _ in perm_parts]
    s_in = [refs.pop(0) for _ in range(elem_parts)]
    e_in = [refs.pop(0) for _ in range(n_slices)]
    out_ref, p_ref, s_ref, e_ref, w_ref, acc_ref, p_sem, s_sem, e_sem = refs
    nv = p_ref.shape[-1]
    ne_part = s_in[0].shape[1]
    ne = s_ref.shape[1]
    n_snk, n_mom = lax.axis_size("snk"), lax.axis_size("mom")
    sep_local = n_sep // n_snk
    seps = sep_local // n_mom
    y, m = lax.axis_index("snk"), lax.axis_index("mom")
    e_copies = [pltpu.make_async_copy(e_in[n], e_ref.at[n], e_sem.at[n]) for n in range(n_slices)]
    p_copies = []
    for n, (dy, dm) in enumerate(perm_parts):
        at = lax.rem(y + dy, n_snk) * sep_local + lax.rem(m + dm, n_mom) * seps
        p_copies.append(pltpu.make_async_copy(p_in[n], p_ref.at[:, pl.ds(at, seps)], p_sem.at[n]))
    s_copies = [
        pltpu.make_async_copy(s_in[n], s_ref.at[:, pl.ds(n * ne_part, ne_part)], s_sem.at[n])
        for n in range(elem_parts)
    ]
    for copy in p_copies + e_copies + s_copies:
        copy.start()
    for copy in p_copies + e_copies:
        copy.wait()

    by_slice = {}
    for n, (c, j, ts) in enumerate(units):
        by_slice.setdefault(c, []).append((n, j, ts))
    for c, group in by_slice.items():
        props = [p_ref[j, ts] for _, j, ts in group]
        stacked = jnp.concatenate(props, axis=0) if len(group) > 1 else props[0]
        halves = [
            jnp.dot(stacked, e_ref[c, f], preferred_element_type=jnp.float32).astype(jnp.bfloat16)
            for f in range(nf)
        ]
        for at, (n, j, ts) in enumerate(group):
            half = jnp.concatenate([h[at * nv : (at + 1) * nv] for h in halves], axis=0)
            sandwich = lax.dot_general(
                half, props[at], (((1,), (1,)), ((), ())), preferred_element_type=jnp.float32
            )
            w_ref[n] = sandwich.astype(jnp.bfloat16).reshape(nf, nv, nv)
    for copy in s_copies:
        copy.wait()

    acc_ref[...] = jnp.zeros_like(acc_ref)
    width = nf * BLK
    for j in range(own):
        group = [(n, ts) for n, (_, jj, ts) in enumerate(units) if jj == j]
        if not group:
            continue
        left = jnp.concatenate(
            [
                jnp.concatenate(
                    [w_ref[n, :, a : a + BLK, :].reshape(width, nv) for n, _ in group], axis=0
                )
                for a in range(0, nv, BLK)
            ],
            axis=1,
        )
        right = jnp.concatenate(
            [s_ref[j, :, a : a + BLK, :].reshape(ne * BLK, nv) for a in range(0, nv, BLK)], axis=1
        )
        part = lax.dot_general(
            left, right, (((1,), (1,)), ((), ())), preferred_element_type=jnp.float32
        )
        for at, (_, ts) in enumerate(group):
            acc_ref[ts * width : (ts + 1) * width] += part[at * width : (at + 1) * width]
    total = acc_ref[...]
    row = lax.broadcasted_iota(jnp.int32, total.shape, 0)
    col = lax.broadcasted_iota(jnp.int32, total.shape, 1)
    kept = jnp.where(lax.rem(row, BLK) == lax.rem(col, BLK), total, 0.0)
    kept = jnp.sum(kept.reshape(n_sep * nf, BLK, ne * BLK), axis=1)
    picked = lax.broadcasted_iota(jnp.int32, (ne * BLK, ne), 0)
    elem = lax.broadcasted_iota(jnp.int32, (ne * BLK, ne), 1)
    group_sum = jnp.where(lax.div(picked, BLK) == elem, 1.0, 0.0).astype(jnp.float32)
    out_ref[...] = jnp.dot(
        kept, group_sum, precision=lax.Precision.HIGHEST, preferred_element_type=jnp.float32
    )


def traces_of(units, slices, perms, elems, n_sep):
    own, ne_part, nv = elems[0].shape[0], elems[0].shape[1], elems[0].shape[2]
    nf = slices[0].shape[0]
    ne = ne_part * len(elems)
    flops = 2 * len(units) * nf * nv * nv * (2 * nv + ne * BLK)
    moved = 2 * nv * nv * (own * n_sep + own * ne + len(slices) * nf)
    return pl.pallas_call(
        functools.partial(
            trace_kernel, units, own, nf, n_sep, tuple(perms), len(elems), len(slices)
        ),
        out_shape=jax.ShapeDtypeStruct((n_sep * nf, ne), jnp.float32),
        in_specs=[ANY] * (len(perms) + len(elems) + len(slices)),
        out_specs=pl.BlockSpec(memory_space=pltpu.VMEM),
        scratch_shapes=[
            pltpu.VMEM((own, n_sep, nv, nv), jnp.bfloat16),
            pltpu.VMEM((own, ne, nv, nv), jnp.bfloat16),
            pltpu.VMEM((len(slices), nf, nv, nv), jnp.bfloat16),
            pltpu.VMEM((len(units), nf, nv, nv), jnp.bfloat16),
            pltpu.VMEM((n_sep * nf * BLK, ne * BLK), jnp.float32),
            pltpu.SemaphoreType.DMA((len(perms),)),
            pltpu.SemaphoreType.DMA((len(elems),)),
            pltpu.SemaphoreType.DMA((len(slices),)),
        ],
        compiler_params=pltpu.CompilerParams(vmem_limit_bytes=56 << 20),
        cost_estimate=pl.CostEstimate(flops=flops, bytes_accessed=moved, transcendentals=0),
    )(*perms.values(), *elems, *slices)


def body(peramb, elem_src, elem_snk, op_elem, hlt_kernel):
    source_count, sep_local, rows, nv = peramb.shape
    n_src, n_snk, n_mom = (lax.axis_size(axis) for axis in ("src", "snk", "mom"))
    s, y, m = (lax.axis_index(axis) for axis in ("src", "snk", "mom"))
    n_sep = sep_local * n_snk
    seps = sep_local // n_mom
    own, ne_part = elem_snk.shape[:2]
    nf = ne_part // n_snk
    highest = lax.Precision.HIGHEST
    even = s % 2 == 0

    quarter = lax.dynamic_slice_in_dim(elem_src, y * nf, nf, 1)
    sheared = shear(peramb, n_src, own, seps)

    def needed(block, i):
        return [(j, own * block + j - i) for j in range(own) if 0 <= own * block + j - i < n_sep]

    reach = -(-(n_sep - 1) // own)
    hops = reach // 2 + 1
    chain = [{i: quarter[i] for i in range(own)}]
    for hop in range(1, hops + 1):
        wanted = [i for i in range(own) if needed(2 * hop - 1, i)]
        chain.append({i: shifted(chain[-1][i], "src", 2) for i in reversed(wanted)})
    blocks = {}
    for block in range(reach + 1):
        for i in reversed(range(own)):
            if not needed(block, i):
                continue
            if block % 2 == 0:
                blocks[block, i] = chain[block // 2][i]
            else:
                low, high = chain[block // 2][i], chain[block // 2 + 1][i]
                blocks[block, i] = swapped(jnp.where(even, low, high), "src")

    rows_in = lax.all_to_all(sheared, "src", 0, 0)
    mine = jnp.transpose(rows_in, (1, 2, 0, 3, 4)).reshape(own, seps, n_src * rows, nv)
    perms = {(0, 0): mine}
    for dy in range(1, n_snk):
        perms[dy, 0] = shifted(mine, "snk", -dy)
    for dy in range(n_snk):
        for dm in range(1, n_mom):
            perms[dy, dm] = shifted(perms[dy, 0], "mom", -dm)
    elems = [elem_snk] + [shifted(elem_snk, "mom", -dm) for dm in range(1, n_mom)]

    order = sorted(blocks, key=lambda b: (b[0] > 0, -b[1]))
    groups = [[b for b in order if b[0] == 0 or b[1] == own - 1]]
    groups += [[b for b in order if b[0] > 0 and b[1] == i] for i in reversed(range(own - 1))]
    total = 0.0
    for group in groups:
        units = [(c, j, ts) for c, (k, i) in enumerate(group) for j, ts in needed(k, i)]
        total = total + traces_of(units, [blocks[b] for b in group], perms, elems, n_sep)

    if n_src == 8:
        for step in (1, 2, 4):
            total = total + lax.ppermute(total, "src", [(i, i ^ step) for i in range(n_src)])
    else:
        total = lax.psum(total, "src")
    gathered = lax.all_gather(total, "snk", axis=0)
    pair_traces = gathered.reshape(n_snk, n_sep, nf, ne_part * n_mom)
    n_ops = op_elem.shape[0] // n_src
    ops = lax.dynamic_slice_in_dim(op_elem, s * n_ops, n_ops, 0)
    names = (jnp.arange(n_mom * ne_part, dtype=jnp.int32) + m * ne_part) % (n_mom * ne_part)
    onehot = (ops[:, None] == names[None, :]).astype(jnp.float32)
    norm_factor = 1.0 / (nv * math.sqrt(source_count))
    correlator = jnp.einsum("oe,ytfe->otyf", onehot, pair_traces, precision=highest) * norm_factor
    correlator = correlator.reshape(n_ops, n_sep, ne_part)
    return jnp.einsum("otf,tk->ofk", correlator, hlt_kernel, precision=highest)


def solution(mesh):
    placed = (
        P(None, "snk", "src", None),
        P("src", "mom", None, None),
        P("src", "mom", None, None),
        P(),
        P(),
    )
    return jax.shard_map(
        body, mesh=mesh, in_specs=placed, out_specs=P("src", "mom", None), check_vma=False
    )
```

```python
import functools
import math

import jax
import jax.numpy as jnp
from jax import lax
from jax.experimental import pallas as pl
from jax.experimental.pallas import tpu as pltpu
from jax.sharding import PartitionSpec as P

BLK = 16
VMEM = pl.BlockSpec(memory_space=pltpu.VMEM)


def shifted(value, axis, steps):
    count = lax.axis_size(axis)
    pairs = [(source, (source + steps) % count) for source in range(count)]
    return lax.ppermute(value, axis, pairs)


def crossed(value, axis, mask):
    count = lax.axis_size(axis)
    return lax.ppermute(value, axis, [(source, source ^ mask) for source in range(count)])


def sent(value, steps, parity=None):
    count = lax.axis_size("src")
    sources = [at for at in range(count) if parity is None or at % 2 == parity]
    return lax.ppermute(value, "src", [(at, (at + steps) % count) for at in sources])


def after(value, *first):
    return lax.optimization_barrier((value, *first))[0]


def shear_kernel(peramb_ref, out_ref):
    source_count, sep_local = peramb_ref.shape[:2]
    n_src, own, seps = out_ref.shape[:3]
    first = lax.axis_index("mom") * seps
    sep0 = lax.axis_index("snk") * sep_local + first
    for d in range(n_src):
        for j in range(own):
            for h in range(seps):
                start = lax.rem(own * d + j - h - sep0 + 2 * source_count, source_count)
                out_ref[d, j, h] = peramb_ref[start, first + h]


def shear(peramb, n_src, own, seps):
    return pl.pallas_call(
        shear_kernel,
        out_shape=jax.ShapeDtypeStruct((n_src, own, seps) + peramb.shape[2:], peramb.dtype),
        in_specs=[VMEM],
        out_specs=VMEM,
        compiler_params=pltpu.CompilerParams(vmem_limit_bytes=16 << 20),
    )(peramb)


def ordered_kernel(parts, *refs):
    *p_in, out_ref = refs
    n_snk, n_mom = lax.axis_size("snk"), lax.axis_size("mom")
    y, m = lax.axis_index("snk"), lax.axis_index("mom")
    own, seps = p_in[0].shape[:2]
    for part, (dy, dm) in zip(p_in, parts):
        at = (lax.rem(y + dy, n_snk) * n_mom + lax.rem(m + dm, n_mom)) * seps
        for j in range(own):
            for h in range(seps):
                out_ref[j, at + h] = part[j, h]


def ordered(perms):
    own, seps, nv = next(iter(perms.values())).shape[:3]
    return pl.pallas_call(
        functools.partial(ordered_kernel, tuple(perms)),
        out_shape=jax.ShapeDtypeStruct((own, seps * len(perms), nv, nv), jnp.bfloat16),
        in_specs=[VMEM] * len(perms),
        out_specs=VMEM,
        compiler_params=pltpu.CompilerParams(vmem_limit_bytes=8 << 20),
    )(*perms.values())


def trace_kernel(units, has_before, elem_parts, slice_parts, last, *refs):
    refs = list(refs)
    before_ref = refs.pop(0) if has_before else None
    p_ref = refs.pop(0)
    s_refs = [refs.pop(0) for _ in range(elem_parts)]
    e_refs = [[refs.pop(0) for _ in range(parts)] for parts in slice_parts]
    out_ref, w_ref, *rest = refs
    acc_ref = rest.pop(0) if last else out_ref
    own, n_sep, nv = p_ref.shape[:3]
    ne_part = s_refs[0].shape[1]
    ne = ne_part * elem_parts
    nf = w_ref.shape[1]
    even = lax.rem(lax.axis_index("src"), 2) == 0
    for c, parts in enumerate(e_refs):
        if len(parts) == 2:
            one, two = parts

            @pl.when(jnp.logical_not(even))
            def _():
                one[...] = two[...]

    for n, (c, j, ts) in enumerate(units):
        prop = p_ref[j, ts]
        for f in range(nf):
            half = jnp.dot(prop, e_refs[c][0][f], preferred_element_type=jnp.float32)
            sandwich = lax.dot_general(
                half.astype(jnp.bfloat16),
                prop,
                (((1,), (1,)), ((), ())),
                preferred_element_type=jnp.float32,
            )
            w_ref[n, f] = sandwich.astype(jnp.bfloat16)

    if has_before:
        acc_ref[...] = before_ref[...]
    else:
        acc_ref[...] = jnp.zeros_like(acc_ref)
    width = nf * BLK
    for j in range(own):
        group = [(n, ts) for n, (_, jj, ts) in enumerate(units) if jj == j]
        if not group:
            continue
        left = jnp.concatenate(
            [
                jnp.concatenate(
                    [w_ref[n, :, a : a + BLK, :].reshape(width, nv) for n, _ in group], axis=0
                )
                for a in range(0, nv, BLK)
            ],
            axis=1,
        )
        right = jnp.concatenate(
            [
                jnp.concatenate(
                    [ref[j, :, a : a + BLK, :].reshape(ne_part * BLK, nv) for ref in s_refs], axis=0
                )
                for a in range(0, nv, BLK)
            ],
            axis=1,
        )
        part = lax.dot_general(
            left, right, (((1,), (1,)), ((), ())), preferred_element_type=jnp.float32
        )
        for at, (_, ts) in enumerate(group):
            acc_ref[ts * width : (ts + 1) * width] += part[at * width : (at + 1) * width]
    if not last:
        return
    total = acc_ref[...]
    row = lax.broadcasted_iota(jnp.int32, total.shape, 0)
    col = lax.broadcasted_iota(jnp.int32, total.shape, 1)
    kept = jnp.where((row & (BLK - 1)) == (col & (BLK - 1)), total, 0.0)
    kept = jnp.sum(kept.reshape(n_sep * nf, BLK, ne * BLK), axis=1)
    picked = lax.broadcasted_iota(jnp.int32, (ne * BLK, ne), 0)
    elem = lax.broadcasted_iota(jnp.int32, (ne * BLK, ne), 1)
    group_sum = jnp.where((picked >> (BLK.bit_length() - 1)) == elem, 1.0, 0.0).astype(jnp.float32)
    out_ref[...] = jnp.dot(
        kept, group_sum, precision=lax.Precision.HIGHEST, preferred_element_type=jnp.float32
    )


def add_traces(before, units, slices, perm, elems, last):
    own, n_sep, nv = perm.shape[:3]
    nf = slices[0][0].shape[0]
    ne = elems[0].shape[1] * len(elems)
    flops = 2 * len(units) * nf * nv * nv * (2 * nv + ne * BLK)
    moved = 2 * nv * nv * (own * n_sep + own * ne + len(slices) * nf)
    slice_parts = [len(parts) for parts in slices]
    flat = [part for parts in slices for part in parts]
    acc = (n_sep * nf * BLK, ne * BLK)
    before = [] if before is None else [before]
    scratch = [pltpu.VMEM((len(units), nf, nv, nv), jnp.bfloat16)]
    if last:
        scratch.append(pltpu.VMEM(acc, jnp.float32))
    return pl.pallas_call(
        functools.partial(trace_kernel, units, bool(before), len(elems), slice_parts, last),
        out_shape=jax.ShapeDtypeStruct((n_sep * nf, ne) if last else acc, jnp.float32),
        in_specs=[VMEM] * (len(before) + 1 + len(elems) + len(flat)),
        out_specs=VMEM,
        scratch_shapes=scratch,
        compiler_params=pltpu.CompilerParams(vmem_limit_bytes=24 << 20),
        cost_estimate=pl.CostEstimate(flops=flops, bytes_accessed=moved, transcendentals=0),
    )(*before, perm, *elems, *flat)


def body(peramb, elem_src, elem_snk, op_elem, hlt_kernel):
    source_count, sep_local, rows, nv = peramb.shape
    n_src, n_snk, n_mom = (lax.axis_size(axis) for axis in ("src", "snk", "mom"))
    s, y, m = (lax.axis_index(axis) for axis in ("src", "snk", "mom"))
    n_sep = sep_local * n_snk
    seps = sep_local // n_mom
    own, ne_part = elem_snk.shape[:2]
    nf = ne_part // n_snk
    highest = lax.Precision.HIGHEST

    def needed(block, i):
        return [(j, own * block + j - i) for j in range(own) if 0 <= own * block + j - i < n_sep]

    reach = -(-(n_sep - 1) // own)
    quarter = lax.dynamic_slice_in_dim(elem_src, y * nf, nf, 1)
    start = [quarter[i] for i in range(own)]
    peramb, *start = lax.optimization_barrier((peramb, *start))
    behind = crossed(start[0], "src", 1)
    sheared = shear(peramb, n_src, own, seps)
    rows_in = lax.all_to_all(sheared, "src", 0, 0)
    start = [after(value, rows_in) for value in start]
    mine = jnp.transpose(rows_in, (1, 2, 0, 3, 4)).reshape(own, seps, n_src * rows, nv)
    blocks = {}
    done = {}
    for i in reversed(range(own)):
        last = max(block for block in range(reach + 1) if needed(block, i))
        chain = [start[i]]
        value = after(start[i], done[i + 2]) if i + 2 in done else start[i]
        while 2 * len(chain) <= last + (1 if i else 0):
            value = sent(value, 2, 1 if 2 * len(chain) > last else None)
            chain.append(value)
        done[i] = chain[1]
        for hop, value in enumerate(chain[: last // 2 + 1]):
            blocks[2 * hop, i] = (value,)
        if i:
            for block in range(1, last + 1, 2):
                low, high = chain[block // 2], chain[block // 2 + 1]
                blocks[block, i] = (sent(high, -1, 1), sent(low, 1, 0))
        else:
            lower = behind
            for block in range(1, last + 1, 2):
                value = after(lower, done[1]) if lower is behind and 1 in done else lower
                upper = sent(value, 2, 0 if block + 2 > last else None)
                blocks[block, i] = (upper, lower)
                lower = upper

    perms = {(0, 0): mine}
    for dy in range(1, n_snk):
        perms[dy, 0] = shifted(mine, "snk", -dy)
    for dy in range(n_snk):
        for dm in range(1, n_mom):
            perms[dy, dm] = shifted(perms[dy, 0], "mom", -dm)
    elems = [elem_snk] + [shifted(elem_snk, "mom", -dm) for dm in range(1, n_mom)]

    groups = [[], [], []]
    for block, i in blocks:
        early = block == 0 or (i == own - 1 and block < 3)
        groups[0 if early else 2 if i == 0 or block > 2 else 1].append((block, i))
    perm = ordered(perms)
    total = None
    for group in groups:
        units = [(c, j, ts) for c, (k, i) in enumerate(group) for j, ts in needed(k, i)]
        slices = [blocks[b] for b in group]
        total = add_traces(total, units, slices, perm, elems, group is groups[-1])

    if n_src == 8:
        for step in (1, 2, 4):
            total = total + crossed(total, "src", step)
    else:
        total = lax.psum(total, "src")
    gathered = lax.all_gather(total, "snk", axis=0)
    pair_traces = gathered.reshape(n_snk, n_sep, nf, ne_part * n_mom)
    n_ops = op_elem.shape[0] // n_src
    ops = lax.dynamic_slice_in_dim(op_elem, s * n_ops, n_ops, 0)
    names = (jnp.arange(n_mom * ne_part, dtype=jnp.int32) + m * ne_part) % (n_mom * ne_part)
    onehot = (ops[:, None] == names[None, :]).astype(jnp.float32)
    norm_factor = 1.0 / (nv * math.sqrt(source_count))
    correlator = jnp.einsum("oe,ytfe->otyf", onehot, pair_traces, precision=highest) * norm_factor
    correlator = correlator.reshape(n_ops, n_sep, ne_part)
    return jnp.einsum("otf,tk->ofk", correlator, hlt_kernel, precision=highest)


def solution(mesh):
    placed = (
        P(None, "snk", "src", None),
        P("src", "mom", None, None),
        P("src", "mom", None, None),
        P(),
        P(),
    )
    return jax.shard_map(
        body, mesh=mesh, in_specs=placed, out_specs=P("src", "mom", None), check_vma=False
    )
```

```python
import functools
import math

import jax
import jax.numpy as jnp
from jax import lax
from jax.experimental import pallas as pl
from jax.experimental.pallas import tpu as pltpu
from jax.sharding import PartitionSpec as P

BLK = 16
VMEM = pl.BlockSpec(memory_space=pltpu.VMEM)


def shifted(value, axis, steps):
    count = lax.axis_size(axis)
    pairs = [(source, (source + steps) % count) for source in range(count)]
    return lax.ppermute(value, axis, pairs)


def crossed(value, axis, mask):
    count = lax.axis_size(axis)
    return lax.ppermute(value, axis, [(source, source ^ mask) for source in range(count)])


def sent(value, steps, parity=None):
    count = lax.axis_size("src")
    sources = [at for at in range(count) if parity is None or at % 2 == parity]
    return lax.ppermute(value, "src", [(at, (at + steps) % count) for at in sources])


def after(value, *first):
    return lax.optimization_barrier((value, *first))[0]


def shear_kernel(peramb_ref, out_ref):
    source_count, sep_local = peramb_ref.shape[:2]
    n_src, own, seps = out_ref.shape[:3]
    first = lax.axis_index("mom") * seps
    sep0 = lax.axis_index("snk") * sep_local + first
    for d in range(n_src):
        for j in range(own):
            for h in range(seps):
                start = lax.rem(own * d + j - h - sep0 + 2 * source_count, source_count)
                out_ref[d, j, h] = peramb_ref[start, first + h]


def shear(peramb, n_src, own, seps):
    return pl.pallas_call(
        shear_kernel,
        out_shape=jax.ShapeDtypeStruct((n_src, own, seps) + peramb.shape[2:], peramb.dtype),
        in_specs=[VMEM],
        out_specs=VMEM,
        compiler_params=pltpu.CompilerParams(vmem_limit_bytes=16 << 20),
    )(peramb)


def ordered_kernel(parts, *refs):
    *p_in, out_ref = refs
    n_snk, n_mom = lax.axis_size("snk"), lax.axis_size("mom")
    y, m = lax.axis_index("snk"), lax.axis_index("mom")
    own, seps = p_in[0].shape[:2]
    for part, (dy, dm) in zip(p_in, parts):
        at = (lax.rem(y + dy, n_snk) * n_mom + lax.rem(m + dm, n_mom)) * seps
        for j in range(own):
            for h in range(seps):
                out_ref[j, at + h] = part[j, h]


def ordered(perms):
    own, seps, nv = next(iter(perms.values())).shape[:3]
    return pl.pallas_call(
        functools.partial(ordered_kernel, tuple(perms)),
        out_shape=jax.ShapeDtypeStruct((own, seps * len(perms), nv, nv), jnp.bfloat16),
        in_specs=[VMEM] * len(perms),
        out_specs=VMEM,
        compiler_params=pltpu.CompilerParams(vmem_limit_bytes=8 << 20),
    )(*perms.values())


def chosen_kernel(even_ref, odd_ref, out_ref):
    even = lax.rem(lax.axis_index("src"), 2) == 0
    for at in range(out_ref.shape[0]):

        @pl.when(even)
        def _():
            out_ref[at] = even_ref[at]

        @pl.when(jnp.logical_not(even))
        def _():
            out_ref[at] = odd_ref[at]


def chosen(for_even, for_odd):
    return pl.pallas_call(
        chosen_kernel,
        out_shape=jax.ShapeDtypeStruct(for_even.shape, for_even.dtype),
        in_specs=[VMEM] * 2,
        out_specs=VMEM,
        compiler_params=pltpu.CompilerParams(vmem_limit_bytes=4 << 20),
    )(for_even, for_odd)


def trace_kernel(units, has_before, elem_parts, n_arrays, slices, last, *refs):
    refs = list(refs)
    before_ref = refs.pop(0) if has_before else None
    p_ref = refs.pop(0)
    s_refs = [refs.pop(0) for _ in range(elem_parts)]
    arrays = [refs.pop(0) for _ in range(n_arrays)]
    out_ref, w_ref, e_ref, *rest = refs
    acc_ref = rest.pop(0) if last else out_ref
    own, n_sep, nv = p_ref.shape[:3]
    ne_part = s_refs[0].shape[1]
    ne = ne_part * elem_parts
    nf = w_ref.shape[1]
    even = lax.rem(lax.axis_index("src"), 2) == 0
    e_refs = []
    merged = 0
    for parts in slices:
        views = [arrays[at] if index is None else arrays[at].at[index] for at, index in parts]
        if len(views) == 2:
            even_view, odd_view = views

            @pl.when(even)
            def _():
                for f in range(nf):
                    e_ref[merged, f] = even_view[f]

            @pl.when(jnp.logical_not(even))
            def _():
                for f in range(nf):
                    e_ref[merged, f] = odd_view[f]

            views = [e_ref.at[merged]]
            merged += 1
        e_refs.append(views[0])

    for n, (c, j, ts) in enumerate(units):
        prop = p_ref[j, ts]
        for f in range(nf):
            half = jnp.dot(prop, e_refs[c][f], preferred_element_type=jnp.float32)
            sandwich = lax.dot_general(
                half.astype(jnp.bfloat16),
                prop,
                (((1,), (1,)), ((), ())),
                preferred_element_type=jnp.float32,
            )
            w_ref[n, f] = sandwich.astype(jnp.bfloat16)

    if has_before:
        acc_ref[...] = before_ref[...]
    else:
        acc_ref[...] = jnp.zeros_like(acc_ref)
    width = nf * BLK
    for j in range(own):
        group = [(n, ts) for n, (_, jj, ts) in enumerate(units) if jj == j]
        if not group:
            continue
        left = jnp.concatenate(
            [
                jnp.concatenate(
                    [w_ref[n, :, a : a + BLK, :].reshape(width, nv) for n, _ in group], axis=0
                )
                for a in range(0, nv, BLK)
            ],
            axis=1,
        )
        right = jnp.concatenate(
            [
                jnp.concatenate(
                    [ref[j, :, a : a + BLK, :].reshape(ne_part * BLK, nv) for ref in s_refs], axis=0
                )
                for a in range(0, nv, BLK)
            ],
            axis=1,
        )
        part = lax.dot_general(
            left, right, (((1,), (1,)), ((), ())), preferred_element_type=jnp.float32
        )
        for at, (_, ts) in enumerate(group):
            acc_ref[ts * width : (ts + 1) * width] += part[at * width : (at + 1) * width]
    if not last:
        return
    total = acc_ref[...]
    row = lax.broadcasted_iota(jnp.int32, total.shape, 0)
    col = lax.broadcasted_iota(jnp.int32, total.shape, 1)
    kept = jnp.where((row & (BLK - 1)) == (col & (BLK - 1)), total, 0.0)
    kept = jnp.sum(kept.reshape(n_sep * nf, BLK, ne * BLK), axis=1)
    picked = lax.broadcasted_iota(jnp.int32, (ne * BLK, ne), 0)
    elem = lax.broadcasted_iota(jnp.int32, (ne * BLK, ne), 1)
    group_sum = jnp.where((picked >> (BLK.bit_length() - 1)) == elem, 1.0, 0.0).astype(jnp.float32)
    out_ref[...] = jnp.dot(
        kept, group_sum, precision=lax.Precision.HIGHEST, preferred_element_type=jnp.float32
    )


def add_traces(before, units, slices, perm, elems, last):
    own, n_sep, nv = perm.shape[:3]
    nf = slices[0][0][0].shape[-3]
    ne = elems[0].shape[1] * len(elems)
    flops = 2 * len(units) * nf * nv * nv * (2 * nv + ne * BLK)
    moved = 2 * nv * nv * (own * n_sep + own * ne + len(slices) * nf)
    arrays, places = [], []
    for parts in slices:
        place = []
        for array, index in parts:
            if not any(array is known for known in arrays):
                arrays.append(array)
            place.append(([array is known for known in arrays].index(True), index))
        places.append(place)
    acc = (n_sep * nf * BLK, ne * BLK)
    before = [] if before is None else [before]
    scratch = [
        pltpu.VMEM((len(units), nf, nv, nv), jnp.bfloat16),
        pltpu.VMEM((max(1, sum(len(parts) > 1 for parts in slices)), nf, nv, nv), jnp.bfloat16),
    ]
    if last:
        scratch.append(pltpu.VMEM(acc, jnp.float32))
    limit = (12 << 20) + 2 * nf * nv * nv * len(units)
    return pl.pallas_call(
        functools.partial(
            trace_kernel, units, bool(before), len(elems), len(arrays), places, last
        ),
        out_shape=jax.ShapeDtypeStruct((n_sep * nf, ne) if last else acc, jnp.float32),
        in_specs=[VMEM] * (len(before) + 1 + len(elems) + len(arrays)),
        out_specs=VMEM,
        scratch_shapes=scratch,
        compiler_params=pltpu.CompilerParams(vmem_limit_bytes=limit),
        cost_estimate=pl.CostEstimate(flops=0, bytes_accessed=1000, transcendentals=0),
    )(*before, perm, *elems, *arrays)


def by_hops(start, needed, reach):
    blocks = {}
    done = {}
    own = len(start)
    behind = crossed(start[0], "src", 1)
    for i in reversed(range(own)):
        last = max(block for block in range(reach + 1) if needed(block, i))
        chain = [start[i]]
        value = after(start[i], done[i + 2]) if i + 2 in done else start[i]
        while 2 * len(chain) <= last + (1 if i else 0):
            value = sent(value, 2, 1 if 2 * len(chain) > last else None)
            chain.append(value)
        done[i] = chain[1]
        for hop, value in enumerate(chain[: last // 2 + 1]):
            blocks[2 * hop, i] = [(value, None)]
        if i:
            for block in range(1, last + 1, 2):
                low, high = chain[block // 2], chain[block // 2 + 1]
                blocks[block, i] = [(sent(high, -1, 1), None), (sent(low, 1, 0), None)]
        else:
            lower = behind
            for block in range(1, last + 1, 2):
                value = after(lower, done[1]) if lower is behind and 1 in done else lower
                upper = sent(value, 2, 0 if block + 2 > last else None)
                blocks[block, i] = [(upper, None), (lower, None)]
                lower = upper
    return blocks


def by_shared_hops(start, later, perm_parts, early):
    first, second, third = start
    two_back = sent(third, 2)
    second_back = sent(second, 2)
    swap_first = crossed(first, "src", 1)
    to_odd = sent(later, 1, 0)
    third_even = sent(two_back, -1, 1)
    onward = sent(after(chosen(swap_first, two_back), *perm_parts), 2)
    second_even = sent(second_back, -1, 1)
    first_back = sent(after(first, second_back), 2)
    blocks = {
        (0, 2): [(third, None)],
        (0, 1): [(second, None)],
        (0, 0): [(first, None)],
        (2, 2): [(two_back, None)],
        (2, 1): [(second_back, None)],
    }
    total = early(blocks)
    last_odd = sent(after(two_back, to_odd, total), 1, 0)
    last_even = sent(after(onward, third_even, second_even, to_odd), -1, 1)
    later_blocks = {
        (1, 2): [(third_even, None), (to_odd, 1)],
        (1, 1): [(second_even, None), (to_odd, 0)],
        (2, 0): [(first_back, None)],
        (1, 0): [(onward, None), (swap_first, None)],
        (3, 2): [(last_even, None), (last_odd, None)],
    }
    return total, later_blocks


def body(peramb, elem_src, elem_snk, op_elem, hlt_kernel):
    source_count, sep_local, rows, nv = peramb.shape
    n_src, n_snk, n_mom = (lax.axis_size(axis) for axis in ("src", "snk", "mom"))
    s, y, m = (lax.axis_index(axis) for axis in ("src", "snk", "mom"))
    n_sep = sep_local * n_snk
    seps = sep_local // n_mom
    own, ne_part = elem_snk.shape[:2]
    nf = ne_part // n_snk
    highest = lax.Precision.HIGHEST

    def needed(block, i):
        return [(j, own * block + j - i) for j in range(own) if 0 <= own * block + j - i < n_sep]

    reach = -(-(n_sep - 1) // own)
    elems = [elem_snk] + [shifted(elem_snk, "mom", -dm) for dm in range(1, n_mom)]
    quarter = lax.dynamic_slice_in_dim(elem_src, y * nf, nf, 1)
    start = [quarter[i] for i in range(own)]
    later = quarter[1:]
    peramb, later, *start = lax.optimization_barrier((peramb, later, *start))
    sheared = shear(peramb, n_src, own, seps)
    rows_in = lax.all_to_all(sheared, "src", 0, 0)
    start = [after(value, rows_in, elems[-1]) for value in start]
    later = after(later, rows_in, elems[-1])
    mine = jnp.transpose(rows_in, (1, 2, 0, 3, 4)).reshape(own, seps, n_src * rows, nv)
    perms = {(dy, 0): shifted(mine, "snk", -dy) if dy else mine for dy in range(n_snk)}
    met = []

    def traces(before, blocks, last=False):
        if not met:
            held = blocks[2, own - 1][0][0]
            for dy in range(n_snk):
                for dm in range(1, n_mom):
                    perms[dy, dm] = shifted(perms[dy, 0], "mom", -dm)
            met.append(ordered(perms))
        units = [(c, j, ts) for c, (k, i) in enumerate(blocks) for j, ts in needed(k, i)]
        return add_traces(before, units, list(blocks.values()), met[0], elems, last)

    if own == 3 and reach == 3 and not needed(3, 1):
        parts = [part for (dy, _), part in perms.items() if dy]
        total, blocks = by_shared_hops(start, later, parts, functools.partial(traces, None))
    else:
        blocks = by_hops(start, needed, reach)
        early = {at: blocks.pop(at) for at in list(blocks) if at[0] == 0 or (at[0] == 2 and at[1])}
        total = traces(None, early)
    next_ones = {at: blocks.pop(at) for at in list(blocks) if at[0] == 1 and at[1]}
    total = traces(total, next_ones)
    total = traces(total, blocks, last=True)

    if n_src == 8:
        for step in (1, 2, 4):
            total = total + crossed(total, "src", step)
    else:
        total = lax.psum(total, "src")
    gathered = lax.all_gather(total, "snk", axis=0)
    pair_traces = gathered.reshape(n_snk, n_sep, nf, ne_part * n_mom)
    n_ops = op_elem.shape[0] // n_src
    ops = lax.dynamic_slice_in_dim(op_elem, s * n_ops, n_ops, 0)
    names = (jnp.arange(n_mom * ne_part, dtype=jnp.int32) + m * ne_part) % (n_mom * ne_part)
    onehot = (ops[:, None] == names[None, :]).astype(jnp.float32)
    norm_factor = 1.0 / (nv * math.sqrt(source_count))
    correlator = jnp.einsum("oe,ytfe->otyf", onehot, pair_traces, precision=highest) * norm_factor
    correlator = correlator.reshape(n_ops, n_sep, ne_part)
    return jnp.einsum("otf,tk->ofk", correlator, hlt_kernel, precision=highest)


def solution(mesh):
    placed = (
        P(None, "snk", "src", None),
        P("src", "mom", None, None),
        P("src", "mom", None, None),
        P(),
        P(),
    )
    return jax.shard_map(
        body, mesh=mesh, in_specs=placed, out_specs=P("src", "mom", None), check_vma=False
    )
```

```python
import functools
import math

import jax
import jax.numpy as jnp
from jax import lax
from jax.experimental import pallas as pl
from jax.experimental.pallas import tpu as pltpu
from jax.sharding import PartitionSpec as P

BLK = 16
VMEM = pl.BlockSpec(memory_space=pltpu.VMEM)


def shifted(value, axis, steps):
    count = lax.axis_size(axis)
    pairs = [(source, (source + steps) % count) for source in range(count)]
    return lax.ppermute(value, axis, pairs)


def crossed(value, axis, mask):
    count = lax.axis_size(axis)
    return lax.ppermute(value, axis, [(source, source ^ mask) for source in range(count)])


def sent(value, steps, parity=None):
    count = lax.axis_size("src")
    sources = [at for at in range(count) if parity is None or at % 2 == parity]
    return lax.ppermute(value, "src", [(at, (at + steps) % count) for at in sources])


def after(value, *first):
    return lax.optimization_barrier((value, *first))[0]


def shear_kernel(peramb_ref, out_ref):
    source_count, sep_local = peramb_ref.shape[:2]
    n_src, own, seps = out_ref.shape[:3]
    first = lax.axis_index("mom") * seps
    sep0 = lax.axis_index("snk") * sep_local + first
    for d in range(n_src):
        for j in range(own):
            for h in range(seps):
                start = lax.rem(own * d + j - h - sep0 + 2 * source_count, source_count)
                out_ref[d, j, h] = peramb_ref[start, first + h]


def shear(peramb, n_src, own, seps):
    return pl.pallas_call(
        shear_kernel,
        out_shape=jax.ShapeDtypeStruct((n_src, own, seps) + peramb.shape[2:], peramb.dtype),
        in_specs=[VMEM],
        out_specs=VMEM,
        compiler_params=pltpu.CompilerParams(vmem_limit_bytes=16 << 20),
    )(peramb)


def ordered_kernel(parts, *refs):
    *p_in, out_ref = refs
    n_snk, n_mom = lax.axis_size("snk"), lax.axis_size("mom")
    y, m = lax.axis_index("snk"), lax.axis_index("mom")
    own, seps = p_in[0].shape[:2]
    for part, (dy, dm) in zip(p_in, parts):
        at = (lax.rem(y + dy, n_snk) * n_mom + lax.rem(m + dm, n_mom)) * seps
        for j in range(own):
            for h in range(seps):
                out_ref[j, at + h] = part[j, h]


def ordered(perms):
    own, seps, nv = next(iter(perms.values())).shape[:3]
    return pl.pallas_call(
        functools.partial(ordered_kernel, tuple(perms)),
        out_shape=jax.ShapeDtypeStruct((own, seps * len(perms), nv, nv), jnp.bfloat16),
        in_specs=[VMEM] * len(perms),
        out_specs=VMEM,
        compiler_params=pltpu.CompilerParams(vmem_limit_bytes=8 << 20),
    )(*perms.values())


def chosen_kernel(even_ref, odd_ref, out_ref):
    even = lax.rem(lax.axis_index("src"), 2) == 0
    for at in range(out_ref.shape[0]):

        @pl.when(even)
        def _():
            out_ref[at] = even_ref[at]

        @pl.when(jnp.logical_not(even))
        def _():
            out_ref[at] = odd_ref[at]


def chosen(for_even, for_odd):
    return pl.pallas_call(
        chosen_kernel,
        out_shape=jax.ShapeDtypeStruct(for_even.shape, for_even.dtype),
        in_specs=[VMEM] * 2,
        out_specs=VMEM,
        compiler_params=pltpu.CompilerParams(vmem_limit_bytes=4 << 20),
    )(for_even, for_odd)


def trace_kernel(units, has_before, elem_parts, n_arrays, slices, last, *refs):
    refs = list(refs)
    before_ref = refs.pop(0) if has_before else None
    p_ref = refs.pop(0)
    s_refs = [refs.pop(0) for _ in range(elem_parts)]
    arrays = [refs.pop(0) for _ in range(n_arrays)]
    out_ref, w_ref, e_ref, *rest = refs
    acc_ref = rest.pop(0) if last else out_ref
    own, n_sep, nv = p_ref.shape[:3]
    ne_part = s_refs[0].shape[1]
    ne = ne_part * elem_parts
    nf = w_ref.shape[1]
    even = lax.rem(lax.axis_index("src"), 2) == 0
    e_refs = []
    merged = 0
    for parts in slices:
        views = [arrays[at] if index is None else arrays[at].at[index] for at, index in parts]
        if len(views) == 2:
            even_view, odd_view = views

            @pl.when(even)
            def _():
                for f in range(nf):
                    e_ref[merged, f] = even_view[f]

            @pl.when(jnp.logical_not(even))
            def _():
                for f in range(nf):
                    e_ref[merged, f] = odd_view[f]

            views = [e_ref.at[merged]]
            merged += 1
        e_refs.append(views[0])

    for n, (c, j, ts) in enumerate(units):
        prop = p_ref[j, ts]
        for f in range(nf):
            half = jnp.dot(prop, e_refs[c][f], preferred_element_type=jnp.float32)
            sandwich = lax.dot_general(
                half.astype(jnp.bfloat16),
                prop,
                (((1,), (1,)), ((), ())),
                preferred_element_type=jnp.float32,
            )
            w_ref[n, f] = sandwich.astype(jnp.bfloat16)

    if has_before:
        acc_ref[...] = before_ref[...]
    else:
        acc_ref[...] = jnp.zeros_like(acc_ref)
    width = nf * BLK
    for j in range(own):
        group = [(n, ts) for n, (_, jj, ts) in enumerate(units) if jj == j]
        if not group:
            continue
        left = jnp.concatenate(
            [
                jnp.concatenate(
                    [w_ref[n, :, a : a + BLK, :].reshape(width, nv) for n, _ in group], axis=0
                )
                for a in range(0, nv, BLK)
            ],
            axis=1,
        )
        right = jnp.concatenate(
            [
                jnp.concatenate(
                    [ref[j, :, a : a + BLK, :].reshape(ne_part * BLK, nv) for ref in s_refs], axis=0
                )
                for a in range(0, nv, BLK)
            ],
            axis=1,
        )
        part = lax.dot_general(
            left, right, (((1,), (1,)), ((), ())), preferred_element_type=jnp.float32
        )
        for at, (_, ts) in enumerate(group):
            acc_ref[ts * width : (ts + 1) * width] += part[at * width : (at + 1) * width]
    if not last:
        return
    total = acc_ref[...]
    row = lax.broadcasted_iota(jnp.int32, total.shape, 0)
    col = lax.broadcasted_iota(jnp.int32, total.shape, 1)
    kept = jnp.where((row & (BLK - 1)) == (col & (BLK - 1)), total, 0.0)
    kept = jnp.sum(kept.reshape(n_sep * nf, BLK, ne * BLK), axis=1)
    picked = lax.broadcasted_iota(jnp.int32, (ne * BLK, ne), 0)
    elem = lax.broadcasted_iota(jnp.int32, (ne * BLK, ne), 1)
    group_sum = jnp.where((picked >> (BLK.bit_length() - 1)) == elem, 1.0, 0.0).astype(jnp.float32)
    out_ref[...] = jnp.dot(
        kept, group_sum, precision=lax.Precision.HIGHEST, preferred_element_type=jnp.float32
    )


def add_traces(before, units, slices, perm, elems, last):
    own, n_sep, nv = perm.shape[:3]
    nf = slices[0][0][0].shape[-3]
    ne = elems[0].shape[1] * len(elems)
    flops = 2 * len(units) * nf * nv * nv * (2 * nv + ne * BLK)
    moved = 2 * nv * nv * (own * n_sep + own * ne + len(slices) * nf)
    arrays, places = [], []
    for parts in slices:
        place = []
        for array, index in parts:
            if not any(array is known for known in arrays):
                arrays.append(array)
            place.append(([array is known for known in arrays].index(True), index))
        places.append(place)
    acc = (n_sep * nf * BLK, ne * BLK)
    before = [] if before is None else [before]
    scratch = [
        pltpu.VMEM((len(units), nf, nv, nv), jnp.bfloat16),
        pltpu.VMEM((max(1, sum(len(parts) > 1 for parts in slices)), nf, nv, nv), jnp.bfloat16),
    ]
    if last:
        scratch.append(pltpu.VMEM(acc, jnp.float32))
    limit = (12 << 20) + 2 * nf * nv * nv * len(units)
    return pl.pallas_call(
        functools.partial(
            trace_kernel, units, bool(before), len(elems), len(arrays), places, last
        ),
        out_shape=jax.ShapeDtypeStruct((n_sep * nf, ne) if last else acc, jnp.float32),
        in_specs=[VMEM] * (len(before) + 1 + len(elems) + len(arrays)),
        out_specs=VMEM,
        scratch_shapes=scratch,
        compiler_params=pltpu.CompilerParams(vmem_limit_bytes=limit),
        cost_estimate=pl.CostEstimate(flops=0, bytes_accessed=1000, transcendentals=0),
    )(*before, perm, *elems, *arrays)


def by_hops(start, needed, reach):
    blocks = {}
    done = {}
    own = len(start)
    behind = crossed(start[0], "src", 1)
    for i in reversed(range(own)):
        last = max(block for block in range(reach + 1) if needed(block, i))
        chain = [start[i]]
        value = after(start[i], done[i + 2]) if i + 2 in done else start[i]
        while 2 * len(chain) <= last + (1 if i else 0):
            value = sent(value, 2, 1 if 2 * len(chain) > last else None)
            chain.append(value)
        done[i] = chain[1]
        for hop, value in enumerate(chain[: last // 2 + 1]):
            blocks[2 * hop, i] = [(value, None)]
        if i:
            for block in range(1, last + 1, 2):
                low, high = chain[block // 2], chain[block // 2 + 1]
                blocks[block, i] = [(sent(high, -1, 1), None), (sent(low, 1, 0), None)]
        else:
            lower = behind
            for block in range(1, last + 1, 2):
                value = after(lower, done[1]) if lower is behind and 1 in done else lower
                upper = sent(value, 2, 0 if block + 2 > last else None)
                blocks[block, i] = [(upper, None), (lower, None)]
                lower = upper
    return blocks


def by_shared_hops(start, later, perm_parts, early):
    first, second, third = start
    two_back = sent(third, 2)
    second_back = sent(second, 2)
    swap_first = crossed(first, "src", 1)
    to_odd = sent(later, 1, 0)
    third_even = sent(two_back, -1, 1)
    onward = sent(after(chosen(swap_first, two_back), *perm_parts), 2)
    second_even = sent(second_back, -1, 1)
    first_back = sent(after(first, second_back), 2)
    blocks = {
        (0, 2): [(third, None)],
        (0, 1): [(second, None)],
        (0, 0): [(first, None)],
        (2, 2): [(two_back, None)],
        (2, 1): [(second_back, None)],
    }
    total = early(blocks)
    last_odd = sent(after(two_back, to_odd, total), 1, 0)
    last_even = sent(after(onward, third_even, second_even, to_odd), -1, 1)
    later_blocks = {
        (1, 2): [(third_even, None), (to_odd, 1)],
        (1, 1): [(second_even, None), (to_odd, 0)],
        (2, 0): [(first_back, None)],
        (1, 0): [(onward, None), (swap_first, None)],
        (3, 2): [(last_even, None), (last_odd, None)],
    }
    return total, later_blocks


def body(peramb, elem_src, elem_snk, op_elem, hlt_kernel):
    source_count, sep_local, rows, nv = peramb.shape
    n_src, n_snk, n_mom = (lax.axis_size(axis) for axis in ("src", "snk", "mom"))
    s, y, m = (lax.axis_index(axis) for axis in ("src", "snk", "mom"))
    n_sep = sep_local * n_snk
    seps = sep_local // n_mom
    own, ne_part = elem_snk.shape[:2]
    nf = ne_part // n_snk
    highest = lax.Precision.HIGHEST

    def needed(block, i):
        return [(j, own * block + j - i) for j in range(own) if 0 <= own * block + j - i < n_sep]

    reach = -(-(n_sep - 1) // own)
    elems = [elem_snk] + [shifted(elem_snk, "mom", -dm) for dm in range(1, n_mom)]
    quarter = lax.dynamic_slice_in_dim(elem_src, y * nf, nf, 1)
    start = [quarter[i] for i in range(own)]
    later = quarter[1:]
    peramb, later, *start = lax.optimization_barrier((peramb, later, *start))
    sheared = shear(peramb, n_src, own, seps)
    rows_in = lax.all_to_all(sheared, "src", 0, 0)
    start = [after(value, rows_in, elems[-1]) for value in start]
    later = after(later, rows_in, elems[-1])
    mine = jnp.transpose(rows_in, (1, 2, 0, 3, 4)).reshape(own, seps, n_src * rows, nv)
    perms = {(dy, 0): shifted(mine, "snk", -dy) if dy else mine for dy in range(n_snk)}
    met = []

    def traces(before, blocks, last=False):
        if not met:
            held = blocks[2, own - 1][0][0]
            for dy in range(n_snk):
                for dm in range(1, n_mom):
                    perms[dy, dm] = shifted(perms[dy, 0], "mom", -dm)
            met.append(ordered(perms))
        units = [(c, j, ts) for c, (k, i) in enumerate(blocks) for j, ts in needed(k, i)]
        return add_traces(before, units, list(blocks.values()), met[0], elems, last)

    if own == 3 and reach == 3 and not needed(3, 1):
        parts = [part for (dy, _), part in perms.items() if dy]
        total, blocks = by_shared_hops(start, later, parts, functools.partial(traces, None))
    else:
        blocks = by_hops(start, needed, reach)
        early = {at: blocks.pop(at) for at in list(blocks) if at[0] == 0 or (at[0] == 2 and at[1])}
        total = traces(None, early)
    next_ones = {at: blocks.pop(at) for at in list(blocks) if at[0] == 1}
    total = traces(total, next_ones)
    total = traces(total, blocks, last=True)

    if n_src == 8:
        for step in (1, 2, 4):
            total = total + crossed(total, "src", step)
    else:
        total = lax.psum(total, "src")
    gathered = lax.all_gather(total, "snk", axis=0)
    pair_traces = gathered.reshape(n_snk, n_sep, nf, ne_part * n_mom)
    n_ops = op_elem.shape[0] // n_src
    ops = lax.dynamic_slice_in_dim(op_elem, s * n_ops, n_ops, 0)
    names = (jnp.arange(n_mom * ne_part, dtype=jnp.int32) + m * ne_part) % (n_mom * ne_part)
    onehot = (ops[:, None] == names[None, :]).astype(jnp.float32)
    norm_factor = 1.0 / (nv * math.sqrt(source_count))
    correlator = jnp.einsum("oe,ytfe->otyf", onehot, pair_traces, precision=highest) * norm_factor
    correlator = correlator.reshape(n_ops, n_sep, ne_part)
    return jnp.einsum("otf,tk->ofk", correlator, hlt_kernel, precision=highest)


def solution(mesh):
    placed = (
        P(None, "snk", "src", None),
        P("src", "mom", None, None),
        P("src", "mom", None, None),
        P(),
        P(),
    )
    return jax.shard_map(
        body, mesh=mesh, in_specs=placed, out_specs=P("src", "mom", None), check_vma=False
    )
```

```python
import functools
import math

import jax
import jax.numpy as jnp
from jax import lax
from jax.experimental import pallas as pl
from jax.experimental.pallas import tpu as pltpu
from jax.sharding import PartitionSpec as P

BLK = 16
VMEM = pl.BlockSpec(memory_space=pltpu.VMEM)


def shifted(value, axis, steps):
    count = lax.axis_size(axis)
    pairs = [(source, (source + steps) % count) for source in range(count)]
    return lax.ppermute(value, axis, pairs)


def crossed(value, axis, mask):
    count = lax.axis_size(axis)
    return lax.ppermute(value, axis, [(source, source ^ mask) for source in range(count)])


def sent(value, steps, parity=None):
    count = lax.axis_size("src")
    sources = [at for at in range(count) if parity is None or at % 2 == parity]
    return lax.ppermute(value, "src", [(at, (at + steps) % count) for at in sources])


def after(value, *first):
    return lax.optimization_barrier((value, *first))[0]


def shear_kernel(peramb_ref, out_ref):
    source_count, sep_local = peramb_ref.shape[:2]
    n_src, own, seps = out_ref.shape[:3]
    first = lax.axis_index("mom") * seps
    sep0 = lax.axis_index("snk") * sep_local + first
    for d in range(n_src):
        for j in range(own):
            for h in range(seps):
                start = lax.rem(own * d + j - h - sep0 + 2 * source_count, source_count)
                out_ref[d, j, h] = peramb_ref[start, first + h]


def shear(peramb, n_src, own, seps):
    return pl.pallas_call(
        shear_kernel,
        out_shape=jax.ShapeDtypeStruct((n_src, own, seps) + peramb.shape[2:], peramb.dtype),
        in_specs=[VMEM],
        out_specs=VMEM,
        compiler_params=pltpu.CompilerParams(vmem_limit_bytes=16 << 20),
    )(peramb)


def ordered_kernel(parts, *refs):
    *p_in, out_ref = refs
    n_snk, n_mom = lax.axis_size("snk"), lax.axis_size("mom")
    y, m = lax.axis_index("snk"), lax.axis_index("mom")
    own, seps = p_in[0].shape[:2]
    for part, (dy, dm) in zip(p_in, parts):
        at = (lax.rem(y + dy, n_snk) * n_mom + lax.rem(m + dm, n_mom)) * seps
        for j in range(own):
            for h in range(seps):
                out_ref[j, at + h] = part[j, h]


def ordered(perms):
    own, seps, nv = next(iter(perms.values())).shape[:3]
    return pl.pallas_call(
        functools.partial(ordered_kernel, tuple(perms)),
        out_shape=jax.ShapeDtypeStruct((own, seps * len(perms), nv, nv), jnp.bfloat16),
        in_specs=[VMEM] * len(perms),
        out_specs=VMEM,
        compiler_params=pltpu.CompilerParams(vmem_limit_bytes=8 << 20),
    )(*perms.values())


def chosen_kernel(even_ref, odd_ref, out_ref):
    even = lax.rem(lax.axis_index("src"), 2) == 0
    for at in range(out_ref.shape[0]):

        @pl.when(even)
        def _():
            out_ref[at] = even_ref[at]

        @pl.when(jnp.logical_not(even))
        def _():
            out_ref[at] = odd_ref[at]


def chosen(for_even, for_odd):
    return pl.pallas_call(
        chosen_kernel,
        out_shape=jax.ShapeDtypeStruct(for_even.shape, for_even.dtype),
        in_specs=[VMEM] * 2,
        out_specs=VMEM,
        compiler_params=pltpu.CompilerParams(vmem_limit_bytes=4 << 20),
    )(for_even, for_odd)


def trace_kernel(units, has_before, elem_parts, n_arrays, slices, last, *refs):
    refs = list(refs)
    before_ref = refs.pop(0) if has_before else None
    p_ref = refs.pop(0)
    s_refs = [refs.pop(0) for _ in range(elem_parts)]
    arrays = [refs.pop(0) for _ in range(n_arrays)]
    out_ref, w_ref, e_ref, *rest = refs
    acc_ref = rest.pop(0) if last else out_ref
    own, n_sep, nv = p_ref.shape[:3]
    ne_part = s_refs[0].shape[1]
    ne = ne_part * elem_parts
    nf = w_ref.shape[1]
    even = lax.rem(lax.axis_index("src"), 2) == 0
    e_refs = []
    merged = 0
    for parts in slices:
        views = [arrays[at] if index is None else arrays[at].at[index] for at, index in parts]
        if len(views) == 2:
            even_view, odd_view = views

            @pl.when(even)
            def _():
                for f in range(nf):
                    e_ref[merged, f] = even_view[f]

            @pl.when(jnp.logical_not(even))
            def _():
                for f in range(nf):
                    e_ref[merged, f] = odd_view[f]

            views = [e_ref.at[merged]]
            merged += 1
        e_refs.append(views[0])

    for n, (c, j, ts) in enumerate(units):
        prop = p_ref[j, ts]
        for f in range(nf):
            half = jnp.dot(prop, e_refs[c][f], preferred_element_type=jnp.float32)
            sandwich = lax.dot_general(
                half.astype(jnp.bfloat16),
                prop,
                (((1,), (1,)), ((), ())),
                preferred_element_type=jnp.float32,
            )
            w_ref[n, f] = sandwich.astype(jnp.bfloat16)

    if has_before:
        acc_ref[...] = before_ref[...]
    else:
        acc_ref[...] = jnp.zeros_like(acc_ref)
    width = nf * BLK
    for j in range(own):
        group = [(n, ts) for n, (_, jj, ts) in enumerate(units) if jj == j]
        if not group:
            continue
        left = jnp.concatenate(
            [
                jnp.concatenate(
                    [w_ref[n, :, a : a + BLK, :].reshape(width, nv) for n, _ in group], axis=0
                )
                for a in range(0, nv, BLK)
            ],
            axis=1,
        )
        right = jnp.concatenate(
            [
                jnp.concatenate(
                    [ref[j, :, a : a + BLK, :].reshape(ne_part * BLK, nv) for ref in s_refs], axis=0
                )
                for a in range(0, nv, BLK)
            ],
            axis=1,
        )
        part = lax.dot_general(
            left, right, (((1,), (1,)), ((), ())), preferred_element_type=jnp.float32
        )
        for at, (_, ts) in enumerate(group):
            acc_ref[ts * width : (ts + 1) * width] += part[at * width : (at + 1) * width]
    if not last:
        return
    total = acc_ref[...]
    row = lax.broadcasted_iota(jnp.int32, total.shape, 0)
    col = lax.broadcasted_iota(jnp.int32, total.shape, 1)
    kept = jnp.where((row & (BLK - 1)) == (col & (BLK - 1)), total, 0.0)
    kept = jnp.sum(kept.reshape(n_sep * nf, BLK, ne * BLK), axis=1)
    picked = lax.broadcasted_iota(jnp.int32, (ne * BLK, ne), 0)
    elem = lax.broadcasted_iota(jnp.int32, (ne * BLK, ne), 1)
    group_sum = jnp.where((picked >> (BLK.bit_length() - 1)) == elem, 1.0, 0.0).astype(jnp.float32)
    out_ref[...] = jnp.dot(
        kept, group_sum, precision=lax.Precision.HIGHEST, preferred_element_type=jnp.float32
    )


def add_traces(before, units, slices, perm, elems, last):
    own, n_sep, nv = perm.shape[:3]
    nf = slices[0][0][0].shape[-3]
    ne = elems[0].shape[1] * len(elems)
    flops = 2 * len(units) * nf * nv * nv * (2 * nv + ne * BLK)
    moved = 2 * nv * nv * (own * n_sep + own * ne + len(slices) * nf)
    arrays, places = [], []
    for parts in slices:
        place = []
        for array, index in parts:
            if not any(array is known for known in arrays):
                arrays.append(array)
            place.append(([array is known for known in arrays].index(True), index))
        places.append(place)
    acc = (n_sep * nf * BLK, ne * BLK)
    before = [] if before is None else [before]
    scratch = [
        pltpu.VMEM((len(units), nf, nv, nv), jnp.bfloat16),
        pltpu.VMEM((max(1, sum(len(parts) > 1 for parts in slices)), nf, nv, nv), jnp.bfloat16),
    ]
    if last:
        scratch.append(pltpu.VMEM(acc, jnp.float32))
    limit = (12 << 20) + 2 * nf * nv * nv * len(units)
    return pl.pallas_call(
        functools.partial(
            trace_kernel, units, bool(before), len(elems), len(arrays), places, last
        ),
        out_shape=jax.ShapeDtypeStruct((n_sep * nf, ne) if last else acc, jnp.float32),
        in_specs=[VMEM] * (len(before) + 1 + len(elems) + len(arrays)),
        out_specs=VMEM,
        scratch_shapes=scratch,
        compiler_params=pltpu.CompilerParams(vmem_limit_bytes=limit),
        cost_estimate=pl.CostEstimate(flops=0, bytes_accessed=1000, transcendentals=0),
    )(*before, perm, *elems, *arrays)


def by_hops(start, needed, reach):
    blocks = {}
    done = {}
    own = len(start)
    behind = crossed(start[0], "src", 1)
    for i in reversed(range(own)):
        last = max(block for block in range(reach + 1) if needed(block, i))
        chain = [start[i]]
        value = after(start[i], done[i + 2]) if i + 2 in done else start[i]
        while 2 * len(chain) <= last + (1 if i else 0):
            value = sent(value, 2, 1 if 2 * len(chain) > last else None)
            chain.append(value)
        done[i] = chain[1]
        for hop, value in enumerate(chain[: last // 2 + 1]):
            blocks[2 * hop, i] = [(value, None)]
        if i:
            for block in range(1, last + 1, 2):
                low, high = chain[block // 2], chain[block // 2 + 1]
                blocks[block, i] = [(sent(high, -1, 1), None), (sent(low, 1, 0), None)]
        else:
            lower = behind
            for block in range(1, last + 1, 2):
                value = after(lower, done[1]) if lower is behind and 1 in done else lower
                upper = sent(value, 2, 0 if block + 2 > last else None)
                blocks[block, i] = [(upper, None), (lower, None)]
                lower = upper
    return blocks


def by_shared_hops(start, later, perm_parts, early):
    first, second, third = start
    two_back = sent(third, 2)
    second_back = sent(second, 2)
    swap_first = crossed(first, "src", 1)
    to_odd = sent(later, 1, 0)
    third_even = sent(two_back, -1, 1)
    onward = sent(after(chosen(swap_first, two_back), *perm_parts), 2)
    second_even = sent(second_back, -1, 1)
    first_back = sent(after(first, second_back), 2)
    blocks = {
        (0, 2): [(third, None)],
        (0, 1): [(second, None)],
        (0, 0): [(first, None)],
        (2, 2): [(two_back, None)],
        (2, 1): [(second_back, None)],
    }
    total = early(blocks)
    last_odd = sent(after(two_back, to_odd, total), 1, 0)
    last_even = sent(after(onward, third_even, second_even, to_odd), -1, 1)
    later_blocks = {
        (1, 2): [(third_even, None), (to_odd, 1)],
        (1, 1): [(second_even, None), (to_odd, 0)],
        (2, 0): [(first_back, None)],
        (1, 0): [(onward, None), (swap_first, None)],
        (3, 2): [(last_even, None), (last_odd, None)],
    }
    return total, later_blocks


def body(peramb, elem_src, elem_snk, op_elem, hlt_kernel):
    source_count, sep_local, rows, nv = peramb.shape
    n_src, n_snk, n_mom = (lax.axis_size(axis) for axis in ("src", "snk", "mom"))
    s, y, m = (lax.axis_index(axis) for axis in ("src", "snk", "mom"))
    n_sep = sep_local * n_snk
    seps = sep_local // n_mom
    own, ne_part = elem_snk.shape[:2]
    nf = ne_part // n_snk
    highest = lax.Precision.HIGHEST

    def needed(block, i):
        return [(j, own * block + j - i) for j in range(own) if 0 <= own * block + j - i < n_sep]

    reach = -(-(n_sep - 1) // own)
    elems = [elem_snk] + [shifted(elem_snk, "mom", -dm) for dm in range(1, n_mom)]
    quarter = lax.dynamic_slice_in_dim(elem_src, y * nf, nf, 1)
    start = [quarter[i] for i in range(own)]
    later = quarter[1:]
    peramb, later, *start = lax.optimization_barrier((peramb, later, *start))
    sheared = shear(peramb, n_src, own, seps)
    rows_in = lax.all_to_all(sheared, "src", 0, 0)
    start = [after(value, rows_in, elems[-1]) for value in start]
    later = after(later, rows_in, elems[-1])
    mine = jnp.transpose(rows_in, (1, 2, 0, 3, 4)).reshape(own, seps, n_src * rows, nv)
    perms = {(dy, 0): shifted(mine, "snk", -dy) if dy else mine for dy in range(n_snk)}
    met = []

    def traces(before, blocks, last=False):
        if not met:
            held = blocks[2, own - 1][0][0]
            for dy in range(n_snk):
                for dm in range(1, n_mom):
                    perms[dy, dm] = shifted(perms[dy, 0], "mom", -dm)
            met.append(ordered(perms))
        units = [(c, j, ts) for c, (k, i) in enumerate(blocks) for j, ts in needed(k, i)]
        return add_traces(before, units, list(blocks.values()), met[0], elems, last)

    if own == 3 and reach == 3 and not needed(3, 1):
        parts = [part for (dy, _), part in perms.items() if dy]
        total, blocks = by_shared_hops(start, later, parts, functools.partial(traces, None))
    else:
        blocks = by_hops(start, needed, reach)
        early = {at: blocks.pop(at) for at in list(blocks) if at[0] == 0 or (at[0] == 2 and at[1])}
        total = traces(None, early)
    next_ones = {at: blocks.pop(at) for at in list(blocks) if at[0] == 1}
    total = traces(total, next_ones)
    total = traces(total, blocks, last=True)

    if n_src == 8 and n_snk == 2:
        pairs = [(at, at ^ 3) for at in range(n_src * n_snk)]
        other = shifted(total, "snk", 1) + lax.ppermute(total, ("src", "snk"), pairs)
        mine = total + crossed(total, "src", 1)
        both = jnp.where(y == 0, jnp.stack([mine, other]), jnp.stack([other, mine]))
        gathered = both + crossed(both, "src", 2) + crossed(both, "src", 4) + crossed(both, "src", 6)
    else:
        gathered = lax.all_gather(lax.psum(total, "src"), "snk", axis=0)
    pair_traces = gathered.reshape(n_snk, n_sep, nf, ne_part * n_mom)
    n_ops = op_elem.shape[0] // n_src
    ops = lax.dynamic_slice_in_dim(op_elem, s * n_ops, n_ops, 0)
    names = (jnp.arange(n_mom * ne_part, dtype=jnp.int32) + m * ne_part) % (n_mom * ne_part)
    onehot = (ops[:, None] == names[None, :]).astype(jnp.float32)
    norm_factor = 1.0 / (nv * math.sqrt(source_count))
    correlator = jnp.einsum("oe,ytfe->otyf", onehot, pair_traces, precision=highest) * norm_factor
    correlator = correlator.reshape(n_ops, n_sep, ne_part)
    return jnp.einsum("otf,tk->ofk", correlator, hlt_kernel, precision=highest)


def solution(mesh):
    placed = (
        P(None, "snk", "src", None),
        P("src", "mom", None, None),
        P("src", "mom", None, None),
        P(),
        P(),
    )
    return jax.shard_map(
        body, mesh=mesh, in_specs=placed, out_specs=P("src", "mom", None), check_vma=False
    )
```

```python
import functools
import math

import jax
import jax.numpy as jnp
from jax import lax
from jax.experimental import pallas as pl
from jax.experimental.pallas import tpu as pltpu
from jax.sharding import PartitionSpec as P

BLK = 16
VMEM = pl.BlockSpec(memory_space=pltpu.VMEM)


def shifted(value, axis, steps):
    count = lax.axis_size(axis)
    pairs = [(source, (source + steps) % count) for source in range(count)]
    return lax.ppermute(value, axis, pairs)


def crossed(value, axis, mask):
    count = lax.axis_size(axis)
    return lax.ppermute(value, axis, [(source, source ^ mask) for source in range(count)])


def sent(value, steps, parity=None):
    count = lax.axis_size("src")
    sources = [at for at in range(count) if parity is None or at % 2 == parity]
    return lax.ppermute(value, "src", [(at, (at + steps) % count) for at in sources])


def after(value, *first):
    return lax.optimization_barrier((value, *first))[0]


def shear_kernel(peramb_ref, out_ref):
    source_count, sep_local = peramb_ref.shape[:2]
    n_src, own, seps = out_ref.shape[:3]
    first = lax.axis_index("mom") * seps
    sep0 = lax.axis_index("snk") * sep_local + first
    for d in range(n_src):
        for j in range(own):
            for h in range(seps):
                start = lax.rem(own * d + j - h - sep0 + 2 * source_count, source_count)
                out_ref[d, j, h] = peramb_ref[start, first + h]


def shear(peramb, n_src, own, seps):
    return pl.pallas_call(
        shear_kernel,
        out_shape=jax.ShapeDtypeStruct((n_src, own, seps) + peramb.shape[2:], peramb.dtype),
        in_specs=[VMEM],
        out_specs=VMEM,
        compiler_params=pltpu.CompilerParams(vmem_limit_bytes=16 << 20),
    )(peramb)


def ordered_kernel(parts, *refs):
    *p_in, out_ref = refs
    n_snk, n_mom = lax.axis_size("snk"), lax.axis_size("mom")
    y, m = lax.axis_index("snk"), lax.axis_index("mom")
    own, seps = p_in[0].shape[:2]
    for part, (dy, dm) in zip(p_in, parts):
        at = (lax.rem(y + dy, n_snk) * n_mom + lax.rem(m + dm, n_mom)) * seps
        for j in range(own):
            for h in range(seps):
                out_ref[j, at + h] = part[j, h]


def ordered(perms):
    own, seps, nv = next(iter(perms.values())).shape[:3]
    return pl.pallas_call(
        functools.partial(ordered_kernel, tuple(perms)),
        out_shape=jax.ShapeDtypeStruct((own, seps * len(perms), nv, nv), jnp.bfloat16),
        in_specs=[VMEM] * len(perms),
        out_specs=VMEM,
        compiler_params=pltpu.CompilerParams(vmem_limit_bytes=8 << 20),
    )(*perms.values())


def chosen_kernel(even_ref, odd_ref, out_ref):
    even = lax.rem(lax.axis_index("src"), 2) == 0
    for at in range(out_ref.shape[0]):

        @pl.when(even)
        def _():
            out_ref[at] = even_ref[at]

        @pl.when(jnp.logical_not(even))
        def _():
            out_ref[at] = odd_ref[at]


def chosen(for_even, for_odd):
    return pl.pallas_call(
        chosen_kernel,
        out_shape=jax.ShapeDtypeStruct(for_even.shape, for_even.dtype),
        in_specs=[VMEM] * 2,
        out_specs=VMEM,
        compiler_params=pltpu.CompilerParams(vmem_limit_bytes=4 << 20),
    )(for_even, for_odd)


def trace_kernel(units, has_before, elem_parts, n_arrays, slices, last, *refs):
    refs = list(refs)
    before_ref = refs.pop(0) if has_before else None
    p_ref = refs.pop(0)
    s_refs = [refs.pop(0) for _ in range(elem_parts)]
    arrays = [refs.pop(0) for _ in range(n_arrays)]
    out_ref, w_ref, e_ref, *rest = refs
    acc_ref = rest.pop(0) if last else out_ref
    own, n_sep, nv = p_ref.shape[:3]
    ne_part = s_refs[0].shape[1]
    ne = ne_part * elem_parts
    nf = w_ref.shape[1]
    even = lax.rem(lax.axis_index("src"), 2) == 0
    e_refs = []
    merged = 0
    for parts in slices:
        views = [arrays[at] if index is None else arrays[at].at[index] for at, index in parts]
        if len(views) == 2:
            even_view, odd_view = views

            @pl.when(even)
            def _():
                for f in range(nf):
                    e_ref[merged, f] = even_view[f]

            @pl.when(jnp.logical_not(even))
            def _():
                for f in range(nf):
                    e_ref[merged, f] = odd_view[f]

            views = [e_ref.at[merged]]
            merged += 1
        e_refs.append(views[0])

    for n, (c, j, ts) in enumerate(units):
        prop = p_ref[j, ts]
        for f in range(nf):
            half = jnp.dot(prop, e_refs[c][f], preferred_element_type=jnp.float32)
            sandwich = lax.dot_general(
                half.astype(jnp.bfloat16),
                prop,
                (((1,), (1,)), ((), ())),
                preferred_element_type=jnp.float32,
            )
            w_ref[n, f] = sandwich.astype(jnp.bfloat16)

    if has_before:
        acc_ref[...] = before_ref[...]
    else:
        acc_ref[...] = jnp.zeros_like(acc_ref)
    width = nf * BLK
    for j in range(own):
        group = [(n, ts) for n, (_, jj, ts) in enumerate(units) if jj == j]
        if not group:
            continue
        left = jnp.concatenate(
            [
                jnp.concatenate(
                    [w_ref[n, :, a : a + BLK, :].reshape(width, nv) for n, _ in group], axis=0
                )
                for a in range(0, nv, BLK)
            ],
            axis=1,
        )
        right = jnp.concatenate(
            [
                jnp.concatenate(
                    [ref[j, :, a : a + BLK, :].reshape(ne_part * BLK, nv) for ref in s_refs], axis=0
                )
                for a in range(0, nv, BLK)
            ],
            axis=1,
        )
        part = lax.dot_general(
            left, right, (((1,), (1,)), ((), ())), preferred_element_type=jnp.float32
        )
        for at, (_, ts) in enumerate(group):
            acc_ref[ts * width : (ts + 1) * width] += part[at * width : (at + 1) * width]
    if not last:
        return
    total = acc_ref[...]
    row = lax.broadcasted_iota(jnp.int32, total.shape, 0)
    col = lax.broadcasted_iota(jnp.int32, total.shape, 1)
    kept = jnp.where((row & (BLK - 1)) == (col & (BLK - 1)), total, 0.0)
    kept = jnp.sum(kept.reshape(n_sep * nf, BLK, ne * BLK), axis=1)
    picked = lax.broadcasted_iota(jnp.int32, (ne * BLK, ne), 0)
    elem = lax.broadcasted_iota(jnp.int32, (ne * BLK, ne), 1)
    group_sum = jnp.where((picked >> (BLK.bit_length() - 1)) == elem, 1.0, 0.0).astype(jnp.float32)
    out_ref[...] = jnp.dot(
        kept, group_sum, precision=lax.Precision.HIGHEST, preferred_element_type=jnp.float32
    )


def add_traces(before, units, slices, perm, elems, last):
    own, n_sep, nv = perm.shape[:3]
    nf = slices[0][0][0].shape[-3]
    ne = elems[0].shape[1] * len(elems)
    flops = 2 * len(units) * nf * nv * nv * (2 * nv + ne * BLK)
    moved = 2 * nv * nv * (own * n_sep + own * ne + len(slices) * nf)
    arrays, places = [], []
    for parts in slices:
        place = []
        for array, index in parts:
            if not any(array is known for known in arrays):
                arrays.append(array)
            place.append(([array is known for known in arrays].index(True), index))
        places.append(place)
    acc = (n_sep * nf * BLK, ne * BLK)
    before = [] if before is None else [before]
    scratch = [
        pltpu.VMEM((len(units), nf, nv, nv), jnp.bfloat16),
        pltpu.VMEM((max(1, sum(len(parts) > 1 for parts in slices)), nf, nv, nv), jnp.bfloat16),
    ]
    if last:
        scratch.append(pltpu.VMEM(acc, jnp.float32))
    limit = (12 << 20) + 2 * nf * nv * nv * len(units)
    return pl.pallas_call(
        functools.partial(
            trace_kernel, units, bool(before), len(elems), len(arrays), places, last
        ),
        out_shape=jax.ShapeDtypeStruct((n_sep * nf, ne) if last else acc, jnp.float32),
        in_specs=[VMEM] * (len(before) + 1 + len(elems) + len(arrays)),
        out_specs=VMEM,
        scratch_shapes=scratch,
        compiler_params=pltpu.CompilerParams(vmem_limit_bytes=limit),
        cost_estimate=pl.CostEstimate(flops=0, bytes_accessed=1000, transcendentals=0),
    )(*before, perm, *elems, *arrays)


def by_hops(start, needed, reach):
    blocks = {}
    done = {}
    own = len(start)
    behind = crossed(start[0], "src", 1)
    for i in reversed(range(own)):
        last = max(block for block in range(reach + 1) if needed(block, i))
        chain = [start[i]]
        value = after(start[i], done[i + 2]) if i + 2 in done else start[i]
        while 2 * len(chain) <= last + (1 if i else 0):
            value = sent(value, 2, 1 if 2 * len(chain) > last else None)
            chain.append(value)
        done[i] = chain[1]
        for hop, value in enumerate(chain[: last // 2 + 1]):
            blocks[2 * hop, i] = [(value, None)]
        if i:
            for block in range(1, last + 1, 2):
                low, high = chain[block // 2], chain[block // 2 + 1]
                blocks[block, i] = [(sent(high, -1, 1), None), (sent(low, 1, 0), None)]
        else:
            lower = behind
            for block in range(1, last + 1, 2):
                value = after(lower, done[1]) if lower is behind and 1 in done else lower
                upper = sent(value, 2, 0 if block + 2 > last else None)
                blocks[block, i] = [(upper, None), (lower, None)]
                lower = upper
    return blocks


def by_shared_hops(start, later, perm_parts, early):
    first, second, third = start
    two_back = sent(third, 2)
    second_back = sent(second, 2)
    swap_first = crossed(first, "src", 1)
    to_odd = sent(later, 1, 0)
    third_even = sent(two_back, -1, 1)
    onward = sent(after(chosen(swap_first, two_back), *perm_parts), 2)
    second_even = sent(second_back, -1, 1)
    first_back = sent(after(first, second_back), 2)
    blocks = {
        (0, 2): [(third, None)],
        (0, 1): [(second, None)],
        (0, 0): [(first, None)],
        (2, 2): [(two_back, None)],
        (2, 1): [(second_back, None)],
    }
    total = early(blocks)
    last_odd = sent(after(two_back, to_odd, total), 1, 0)
    last_even = sent(after(onward, third_even, second_even, to_odd), -1, 1)
    later_blocks = {
        (1, 2): [(third_even, None), (to_odd, 1)],
        (1, 1): [(second_even, None), (to_odd, 0)],
        (2, 0): [(first_back, None)],
        (1, 0): [(onward, None), (swap_first, None)],
        (3, 2): [(last_even, None), (last_odd, None)],
    }
    return total, later_blocks


def body(peramb, elem_src, elem_snk, op_elem, hlt_kernel):
    source_count, sep_local, rows, nv = peramb.shape
    n_src, n_snk, n_mom = (lax.axis_size(axis) for axis in ("src", "snk", "mom"))
    s, y, m = (lax.axis_index(axis) for axis in ("src", "snk", "mom"))
    n_sep = sep_local * n_snk
    seps = sep_local // n_mom
    own, ne_part = elem_snk.shape[:2]
    nf = ne_part // n_snk
    highest = lax.Precision.HIGHEST

    def needed(block, i):
        return [(j, own * block + j - i) for j in range(own) if 0 <= own * block + j - i < n_sep]

    reach = -(-(n_sep - 1) // own)
    elems = [elem_snk] + [shifted(elem_snk, "mom", -dm) for dm in range(1, n_mom)]
    quarter = lax.dynamic_slice_in_dim(elem_src, y * nf, nf, 1)
    start = [quarter[i] for i in range(own)]
    later = quarter[1:]
    peramb, later, *start = lax.optimization_barrier((peramb, later, *start))
    sheared = shear(peramb, n_src, own, seps)
    rows_in = lax.all_to_all(sheared, "src", 0, 0)
    start = [after(value, rows_in, elems[-1]) for value in start]
    later = after(later, rows_in, elems[-1])
    mine = jnp.transpose(rows_in, (1, 2, 0, 3, 4)).reshape(own, seps, n_src * rows, nv)
    perms = {(dy, 0): shifted(mine, "snk", -dy) if dy else mine for dy in range(n_snk)}
    met = []

    def traces(before, blocks, last=False):
        if not met:
            held = blocks[2, own - 1][0][0]
            for dy in range(n_snk):
                for dm in range(1, n_mom):
                    perms[dy, dm] = shifted(perms[dy, 0], "mom", -dm)
            met.append(ordered(perms))
        units = [(c, j, ts) for c, (k, i) in enumerate(blocks) for j, ts in needed(k, i)]
        return add_traces(before, units, list(blocks.values()), met[0], elems, last)

    if own == 3 and reach == 3 and not needed(3, 1):
        parts = [part for (dy, _), part in perms.items() if dy]
        total, blocks = by_shared_hops(start, later, parts, functools.partial(traces, None))
    else:
        blocks = by_hops(start, needed, reach)
        early = {at: blocks.pop(at) for at in list(blocks) if at[0] == 0 or (at[0] == 2 and at[1])}
        total = traces(None, early)
    next_ones = {at: blocks.pop(at) for at in list(blocks) if at[0] == 1}
    total = traces(total, next_ones)
    total = traces(total, blocks, last=True)

    if n_src == 8 and n_snk == 2:
        pairs = [(at, at ^ 3) for at in range(n_src * n_snk)]
        other = shifted(total, "snk", 1) + lax.ppermute(total, ("src", "snk"), pairs)
        mine = total + crossed(total, "src", 1)
        both = jnp.where(y == 0, jnp.stack([mine, other]), jnp.stack([other, mine]))
        both = both + crossed(both, "src", 2)
        gathered = both + crossed(both, "src", 4)
    else:
        gathered = lax.all_gather(lax.psum(total, "src"), "snk", axis=0)
    pair_traces = gathered.reshape(n_snk, n_sep, nf, ne_part * n_mom)
    n_ops = op_elem.shape[0] // n_src
    ops = lax.dynamic_slice_in_dim(op_elem, s * n_ops, n_ops, 0)
    names = (jnp.arange(n_mom * ne_part, dtype=jnp.int32) + m * ne_part) % (n_mom * ne_part)
    onehot = (ops[:, None] == names[None, :]).astype(jnp.float32)
    norm_factor = 1.0 / (nv * math.sqrt(source_count))
    correlator = jnp.einsum("oe,ytfe->otyf", onehot, pair_traces, precision=highest) * norm_factor
    correlator = correlator.reshape(n_ops, n_sep, ne_part)
    return jnp.einsum("otf,tk->ofk", correlator, hlt_kernel, precision=highest)


def solution(mesh):
    placed = (
        P(None, "snk", "src", None),
        P("src", "mom", None, None),
        P("src", "mom", None, None),
        P(),
        P(),
    )
    return jax.shard_map(
        body, mesh=mesh, in_specs=placed, out_specs=P("src", "mom", None), check_vma=False
    )
```
